256 devices in a mesh: fsdp: 64 (over x, y_hi, z), tp: 4 (over y_lo, core).
Axes of the slice: x: 4, y: 4 (y_hi: 2, y_lo: 2; y = y_hi * 2 + y_lo), z: 8, core: 2. Of those that a mesh axis runs over, the one named last changes fastest.
Arguments:
- activations: bfloat16 [32768, 8192], P('fsdp', 'tp'), may hold values from -6 to 6
- cotangent: bfloat16 [32768, 8192], P('fsdp', 'tp'), may hold values from -0.09375 to 0.09375
- projector: bfloat16 [8192, 1024], P(None, 'tp'), may hold values from -0.0625 to 0.0625
- first_moment: float32 [8192, 1024], P('fsdp', 'tp'), may hold values from -6 to 6
- second_moment: float32 [8192, 1024], P('fsdp', 'tp'), may hold values from 0.25 to 4
Outputs:
- weight_update: float32 [8192, 8192], P('tp', 'fsdp')
- first_new: float32 [8192, 1024], P('fsdp', 'tp')
- second_new: float32 [8192, 1024], P('fsdp', 'tp')
The draws below stay inside these ranges and needn't reach their ends.
All inputs are finite; a program needn't handle non-finite values.
Results may differ from the reference program's by a relative error of at most 0.0029.
Values may be sent and summed in bfloat16 or wider, within the bound.
A program may use at most 128 MiB of HBM per device.

```python
import math
import jax
import jax.numpy as jnp

D = 8192
RANK = 1024
TOKENS = 32768


def raised(array, rng, source, target, blocks, factor):
    owner, partner = [(jnp.arange(array.shape[axis_at]) // (array.shape[axis_at] // blocks)).reshape([-1 if axis == axis_at else 1 for axis in range(array.ndim)]) for axis_at in (source, target)]
    chosen = jax.random.permutation(rng, blocks)[partner]
    strong = (owner == chosen) | (owner == (partner + blocks // 2) % blocks)
    return jnp.where(strong, factor * array, array)


def block_scale(own_key, shape, split, least, largest):
    def one(axis_at, shards_of):
        steps = jax.random.uniform(jax.random.fold_in(jax.random.fold_in(own_key, 6), axis_at), (shards_of,), jnp.float32, least / len(split), largest / len(split))
        return jnp.repeat(jnp.exp(steps), shape[axis_at] // shards_of).reshape((-1,) + (1,) * (len(shape) - axis_at - 1))

    factor_of = one(*split[0])
    for cut in split[1:]:
        factor_of = factor_of * one(*cut)
    return factor_of


def bell_draw(key, extent, deviation, bound, shards=(), dtype=jnp.bfloat16):
    entries = jax.random.normal(key, extent, jnp.float32) * deviation
    if len(shards) > 0:
        entries = block_scale(key, extent, shards, -0.22, 0.18) * entries
    return jnp.clip(entries, min=-bound, max=bound).astype(dtype)


def bell_draw_with(stream_key, extent, deviation, reach, pieces, heavy, held_as=jnp.bfloat16):
    values = deviation * jax.random.normal(stream_key, extent, jnp.float32)
    if pieces:
        values = values * block_scale(stream_key, extent, pieces, -0.22, 0.18)
    return jnp.clip(raised(values, jax.random.fold_in(stream_key, 3), *heavy), -reach, reach).astype(held_as)


def setup_inputs(seed: int = 0) -> dict:
    key_list = jax.random.split(jax.random.key(seed), 6)
    return {
        "activations": bell_draw(key_list[0], (TOKENS, D), 1.0, 6.0, ((0, 64), (1, 4))),
        "cotangent": bell_draw_with(key_list[1], (TOKENS, D), (TOKENS ** -0.5), 0.09375, ((0, 64), (1, 4)), (0, 1, 64, 4.0)),
        "projector": bell_draw(key_list[2], (D, RANK), D ** -0.5, 0.0625, ((1, 4),)),
        "first_moment": bell_draw(key_list[3], (D, RANK), 1.0, 6.0, ((0, 64), (1, 4)), jnp.float32),
        "second_moment": jnp.clip(jnp.exp(math.log(4.0) - 2.7725887 * jax.random.uniform(key_list[4], (D, RANK), jnp.float32) ** block_scale(key_list[4], (D, RANK), ((0, 64), (1, 4)), -0.2, 0.2)), 0.25, 4.0),
    }


def reference(activations, cotangent, projector, first_moment, second_moment):
    projected = jnp.dot(activations, projector, preferred_element_type=jnp.float32).astype(jnp.bfloat16)
    grad_proj = jnp.dot(cotangent.T, projected, preferred_element_type=jnp.float32)
    first_new = 0.9 * first_moment + 0.1 * grad_proj
    second_new = 0.999 * second_moment + 0.001 * grad_proj * grad_proj
    direction = (first_new / (jnp.sqrt(second_new) + 1e-08)).astype(jnp.bfloat16)
    weight_update = jnp.dot(projector, direction.T, preferred_element_type=jnp.float32)
    return (weight_update, first_new, second_new)
```

```python
import jax
import jax.numpy as jnp
from jax import lax
from jax.experimental import pallas as pl
from jax.experimental.pallas import tpu as pltpu
from jax.sharding import PartitionSpec as P

MESH = pl.DeviceIdType.MESH
BF, F32 = jnp.bfloat16, jnp.float32
WA, WB = 64, 64


def device(x, y_hi, z, t):
    return (x * 16 + y_hi * 8 + z, t)


def kernel(
    a_hbm, c_hbm, p_hbm, m1_hbm, m2_hbm,
    w_out, f_out, s_out,
    a_v, c_v, ct_v, p_v, m1_v, m2_v,
    hold, core_out, core_in, y_out, y_in, proj,
    ga, gb, xin, fa, zb1, zb2, za1, za2, fb, ra, rb, dirs,
    lsem, psend, precv, esend, erecv, xsend, xrecv,
    zbsend, zbrecv, zasend, zarecv, rasend, rarecv, rbsend, rbrecv, dsend, drecv,
):
    f = lax.axis_index("fsdp")
    t = lax.axis_index("tp")
    x, y_hi, z = f // 16, (f // 8) % 2, f % 8
    y_lo, c = t // 2, t % 2
    y = y_hi * 2 + y_lo

    def at_y(step, core):
        yy = lax.rem(y + step + 4, 4)
        return device(x, yy // 2, z, (yy % 2) * 2 + core)

    def at_x(step):
        return device(lax.rem(x + step + 4, 4), y_hi, z, t)

    def at_z(step):
        return device(x, y_hi, lax.rem(z + step + 8, 8), t)

    other_core = device(x, y_hi, z, y_lo * 2 + 1 - c)
    y_partner = device(x, y_hi, z, (1 - y_lo) * 2 + c)

    def remote(src, dst, ss, rs, dev):
        return pltpu.make_async_remote_copy(
            src_ref=src, dst_ref=dst, send_sem=ss, recv_sem=rs, device_id=dev, device_id_type=MESH
        )

    even = x % 2 == 0
    inner = (x == 0) | (x == 3)
    pairs = [
        (jnp.where(inner, 1, 0), jnp.where(inner, 2, 3)),
        (jnp.where(inner, 0, 1), jnp.where(inner, 3, 2)),
    ]

    loads = [
        pltpu.make_async_copy(a_hbm, a_v, lsem.at[0]),
        pltpu.make_async_copy(c_hbm, c_v, lsem.at[1]),
        pltpu.make_async_copy(p_hbm.at[pl.ds(t * 2048, 2048)], p_v.at[t], lsem.at[2]),
        pltpu.make_async_copy(m1_hbm, m1_v, lsem.at[3]),
        pltpu.make_async_copy(m2_hbm, m2_v, lsem.at[4]),
    ]
    for load in loads:
        load.start()

    barrier = pltpu.get_barrier_semaphore()
    partners = [other_core, at_x(1), at_x(-1), at_z(1), at_z(-1)]
    partners += [at_y(s, k) for s in (1, -1) for k in (0, 1)]
    for dev in partners:
        pl.semaphore_signal(barrier, inc=1, device_id=dev, device_id_type=MESH)
    for xs in range(4):
        for yh in range(2):
            @pl.when(jnp.logical_not((xs == x) & (x == t) & (yh == y_hi)))
            def _():
                pl.semaphore_signal(
                    barrier, inc=1, device_id=device(xs, yh, z, x), device_id_type=MESH
                )

    pl.semaphore_wait(barrier, len(partners) + 8 - jnp.where(x == t, 1, 0))

    p_core = remote(
        p_hbm.at[pl.ds((y_lo * 2 + 1 - c) * 2048, 2048)], p_v.at[t], psend.at[4], precv.at[4], other_core
    )
    p_core.start()

    def p_send(side, core):
        base = ((1 - y_lo) * 2 + core) * 2048 + side * 1024
        return remote(
            p_hbm.at[pl.ds(base, 1024)],
            p_v.at[t, pl.ds(side * 1024, 1024)],
            psend.at[side * 2 + core],
            precv.at[side * 2 + c],
            at_y(1 if side == 0 else -1, core),
        )

    def p_recv(side, core_from):
        slot = p_v.at[(1 - y_lo) * 2 + core_from, pl.ds(side * 1024, 1024)]
        return remote(slot, slot, psend.at[0], precv.at[side * 2 + core_from], other_core)

    def p_sends(h):
        own = (pairs[h][0] == t) | (pairs[h][1] == t)

        @pl.when(own)
        def _():
            for side in range(2):
                for core in range(2):
                    p_send(side, core).start()

    p_sends(0)

    loads[1].wait()

    @pl.loop(0, 8)
    def _(i):
        o = pl.multiple_of(i * 256, 256)
        ct_v[pl.ds(o, 256), :] = c_v[:, pl.ds(o, 256)].T

    loads[0].wait()
    loads[2].wait()

    def dot_partial(q, keep):
        @pl.loop(0, 2)
        def _(i):
            rows = pl.ds(pl.multiple_of(i * 256, 256), 256)
            acc = jnp.dot(a_v[rows, :], p_v[q], preferred_element_type=F32)
            if keep:
                hold[rows, :] = acc
            else:
                core_out[rows, :] = acc.astype(BF)

    def project(h):
        mine = pairs[h]
        q_local = jnp.where(y_lo == 0, mine[0], mine[1])
        q_far = jnp.where(y_lo == 0, mine[1], mine[0])
        to_core = remote(core_out, core_in.at[h], esend.at[h, 0], erecv.at[h, 0], other_core)
        to_y = remote(y_out.at[h], y_in.at[h], esend.at[h, 1], erecv.at[h, 1], y_partner)
        to_core2 = remote(proj.at[h, c], proj.at[h, c], esend.at[h, 2], erecv.at[h, 2], other_core)

        def keep_and_send(q):
            dot_partial(q, True)
            to_core.wait_recv()
            hold[...] = hold[...] + core_in[h].astype(F32)
            y_out[h] = hold[...].astype(BF)
            to_y.start()

        def give(q):
            dot_partial(q, False)
            to_core.start()

        first = c == y_lo
        if h == 0:
            @pl.when(q_local != t)
            def _():
                p_core.wait_recv()
        else:
            @pl.when(q_local != t)
            def _():
                p_core.wait_recv()

        @pl.when(first)
        def _():
            keep_and_send(q_local)

        @pl.when(jnp.logical_not(first))
        def _():
            give(q_local)

        far_core = q_far % 2
        for side in range(2):
            p_recv(side, far_core).wait_recv()
        if h == 0:
            p_sends(1)

        @pl.when(first)
        def _():
            give(q_far)

        @pl.when(jnp.logical_not(first))
        def _():
            keep_and_send(q_far)

        to_y.wait_recv()
        proj[h, c] = (hold[...] + y_in[h].astype(F32)).astype(BF)
        to_core2.start()
        to_core.wait_send()
        to_core2.wait_recv()
        return to_y, to_core2

    def gradient(h, slot):
        q = pairs[h][slot]

        @pl.loop(0, 8)
        def _(i):
            rows = pl.ds(pl.multiple_of(i * 256, 256), 256)
            acc = jnp.dot(ct_v[rows, :], proj[h, slot], preferred_element_type=F32)
            both = acc.astype(BF).reshape(2, 128, 256)
            for k in range(2):
                j = i * 2 + k
                ga[q, j] = both[k, :WA]
                gb[h, j % 8, j // 8, slot] = both[k, WA:]

    def half_of(d):
        return d

    def xq(d, n):
        step = jnp.where(d == 0, n, -n)
        return lax.rem(x + step + 4, 4)

    def x_to(d):
        return device(lax.rem(x + jnp.where(d == 0, 1, 3), 4), y_hi, z, t)

    def x_msg(d, m):
        if m == 0:
            q, half = xq(d, 2), d
        elif m == 1:
            q, half = xq(d, 1), 1 - d
        else:
            q, half = xq(d, 1), d
        src = ga.at[q, pl.ds(half * 8, 8)]
        return remote(src, xin.at[d, m], xsend.at[d, m], xrecv.at[d, m], x_to(d))

    def x_sum(d):
        x_msg(d, 0).wait_recv()
        q = xq(d, 1)
        for k in range(8):
            j = d * 8 + k
            ga[q, j] = (ga[q, j].astype(F32) + xin[d, 0, k].astype(F32)).astype(BF)
        x_msg(d, 2).start()

    def zc(d, n):
        return lax.rem(z + (n if d == 0 else 8 - n), 8)

    def zb_msg(h, d, m):
        if m == 0:
            return remote(
                gb.at[h, zc(d, 4), d], zb1.at[h, d], zbsend.at[h, d, 0], zbrecv.at[h, d, 0],
                at_z(1 if d == 0 else -1),
            )
        return remote(
            gb.at[h, zc(d, 4 - m)], zb2.at[h, d, m - 1], zbsend.at[h, d, m], zbrecv.at[h, d, m],
            at_z(1 if d == 0 else -1),
        )

    def zb_step(h, d, m):
        zb_msg(h, d, m - 1).wait_recv()
        if m == 1:
            tgt = gb.at[h, zc(d, 3), d]
            tgt[...] = (tgt[...].astype(F32) + zb1[h, d].astype(F32)).astype(BF)
        else:
            tgt = gb.at[h, zc(d, 4 - m)]
            tgt[...] = (tgt[...].astype(F32) + zb2[h, d, m - 2].astype(F32)).astype(BF)
        zb_msg(h, d, m).start()

    def za_msg(d, m):
        if m == 0:
            return remote(
                fa.at[zc(d, 4), d], za1.at[d], zasend.at[d, 0], zarecv.at[d, 0],
                at_z(1 if d == 0 else -1),
            )
        return remote(
            fa.at[zc(d, 4 - m)], za2.at[d, m - 1], zasend.at[d, m], zarecv.at[d, m],
            at_z(1 if d == 0 else -1),
        )

    def za_step(d, m):
        za_msg(d, m - 1).wait_recv()
        if m == 1:
            tgt = fa.at[zc(d, 3), d]
            tgt[...] = (tgt[...].astype(F32) + za1[d].astype(F32)).astype(BF)
        else:
            tgt = fa.at[zc(d, 4 - m)]
            tgt[...] = (tgt[...].astype(F32) + za2[d, m - 2].astype(F32)).astype(BF)
        za_msg(d, m).start()

    def mine_a(yh):
        return (x == t) & (yh == y_hi)

    def mine_b(yh, q):
        return (x == t) & (yh == y_hi) & (q == t)

    def ra_msg(yh):
        return remote(fa.at[z, yh], ra.at[y_hi], rasend.at[yh], rarecv.at[y_hi], device(t, yh, z, x))

    def rb_msg(h, slot, yh):
        q = pairs[h][slot]
        return remote(
            fb.at[h, yh, slot], rb.at[x * 2 + y_hi], rbsend.at[h, slot, yh], rbrecv.at[x * 2 + y_hi],
            device(t, yh, z, q),
        )

    def zb_final(h):
        for d in range(2):
            zb_msg(h, d, 3).wait_recv()
        fb[h] = (
            gb[h, z].astype(F32) + zb2[h, 0, 2].astype(F32) + zb2[h, 1, 2].astype(F32)
        ).astype(BF)
        for slot in range(2):
            q = pairs[h][slot]
            for yh in range(2):
                own = mine_b(yh, q)

                @pl.when(own)
                def _():
                    rb[x * 2 + y_hi] = fb[h, yh, slot]

                @pl.when(jnp.logical_not(own))
                def _():
                    rb_msg(h, slot, yh).start()

    exch0 = project(0)
    first_slot = lax.rem(x + 2, 4)
    for slot in range(2):
        gradient(0, slot)
    near = jnp.where(even, 0, 1)
    far = 1 - near
    for d in range(2):
        x_msg(d, 0).start()
        zb_msg(0, d, 0).start()
    x_msg(near, 1).start()
    exch1 = project(1)
    x_sum(near)
    for d in range(2):
        zb_step(0, d, 1)
    for slot in range(2):
        gradient(1, slot)
    x_msg(far, 1).start()
    x_sum(far)
    for d in range(2):
        zb_msg(1, d, 0).start()
    for m in (2, 3):
        for d in range(2):
            zb_step(0, d, m)
        for d in range(2):
            zb_step(1, d, m - 1)
    for d in range(2):
        zb_step(1, d, 3)
    zb_final(0)

    for d in range(2):
        x_msg(d, 1).wait_recv()
        x_msg(d, 2).wait_recv()
    for yh in range(2):
        for k in range(8):
            fa[k, yh] = (
                ga[x, yh * 8 + k].astype(F32)
                + xin[yh, 2, k].astype(F32)
                + xin[1 - yh, 1, k].astype(F32)
            ).astype(BF)
    for d in range(2):
        za_msg(d, 0).start()
    zb_final(1)
    for m in (1, 2, 3):
        for d in range(2):
            za_step(d, m)
    for d in range(2):
        za_msg(d, 3).wait_recv()
    fa[z] = (fa[z].astype(F32) + za2[0, 2].astype(F32) + za2[1, 2].astype(F32)).astype(BF)
    for yh in range(2):
        own = mine_a(yh)

        @pl.when(own)
        def _():
            ra[y_hi] = fa[z, yh]

        @pl.when(jnp.logical_not(own))
        def _():
            ra_msg(yh).start()

    def ra_wait(s):
        remote(ra.at[s], ra.at[s], rasend.at[0], rarecv.at[s], other_core).wait_recv()

    def rb_wait(s):
        remote(rb.at[s], rb.at[s], rbsend.at[0, 0, 0], rbrecv.at[s], other_core).wait_recv()

    for xs in range(4):
        for yh in range(2):
            @pl.when(jnp.logical_not((xs == x) & (x == t) & (yh == y_hi)))
            def _():
                rb_wait(xs * 2 + yh)
    for yh in range(2):
        @pl.when(jnp.logical_not(mine_a(yh)))
        def _():
            ra_wait(yh)

    loads[3].wait()
    loads[4].wait()
    up = ra[0].astype(F32) + ra[1].astype(F32)
    down = rb[0].astype(F32)
    for s in range(1, 8):
        down = down + rb[s].astype(F32)
    for rows, g in ((pl.ds(0, WA), up), (pl.ds(WA, WB), down)):
        first_new = 0.9 * m1_v[rows, :] + 0.1 * g
        second_new = 0.999 * m2_v[rows, :] + 0.001 * g * g
        f_out[rows, :] = first_new
        s_out[rows, :] = second_new
        dirs[t, rows, :] = (first_new / (jnp.sqrt(second_new) + 1e-08)).astype(BF)

    def d_msg(k):
        return remote(
            dirs.at[t], dirs.at[t], dsend.at[k], drecv.at[k], (f, lax.rem(t + k, 4))
        )

    def d_wait(k):
        slot = dirs.at[lax.rem(t + 4 - k, 4)]
        remote(slot, slot, dsend.at[k], drecv.at[k], other_core).wait_recv()

    for k in (1, 2, 3):
        d_msg(k).start()
    for k in (1, 2, 3):
        d_wait(k)

    @pl.loop(0, 8)
    def _(i):
        rows = pl.ds(pl.multiple_of(i * 256, 256), 256)
        acc = jnp.zeros((256, 128), F32)
        for q in range(4):
            acc = acc + lax.dot_general(
                p_v[q, rows, :], dirs[q], (((1,), (1,)), ((), ())), preferred_element_type=F32
            )
        w_out[rows, :] = acc

    p_core.wait_send()
    for side in range(2):
        for core in range(2):
            p_send(side, core).wait_send()
    for to_y, to_core2 in (exch0, exch1):
        to_y.wait_send()
        to_core2.wait_send()
    for d in range(2):
        for m in range(3):
            x_msg(d, m).wait_send()
        for m in range(4):
            zb_msg(0, d, m).wait_send()
            zb_msg(1, d, m).wait_send()
            za_msg(d, m).wait_send()
    for yh in range(2):
        @pl.when(jnp.logical_not(mine_a(yh)))
        def _():
            ra_msg(yh).wait_send()

        for h in range(2):
            for slot in range(2):
                @pl.when(jnp.logical_not(mine_b(yh, pairs[h][slot])))
                def _():
                    rb_msg(h, slot, yh).wait_send()
    for k in (1, 2, 3):
        d_msg(k).wait_send()


def body(activations, cotangent, projector, first_moment, second_moment):
    dma = pltpu.SemaphoreType.DMA
    vm = pltpu.VMEM
    return pl.pallas_call(
        kernel,
        name="galore_step",
        out_shape=(
            jax.ShapeDtypeStruct((2048, 128), F32),
            jax.ShapeDtypeStruct((128, 256), F32),
            jax.ShapeDtypeStruct((128, 256), F32),
        ),
        in_specs=[pl.BlockSpec(memory_space=pl.ANY)] * 5,
        out_specs=(pl.BlockSpec(memory_space=pltpu.VMEM),) * 3,
        scratch_shapes=[
            vm((512, 2048), BF),
            vm((512, 2048), BF),
            vm((2048, 512), BF),
            vm((4, 2048, 256), BF),
            vm((128, 256), F32),
            vm((128, 256), F32),
            vm((512, 256), F32),
            vm((512, 256), BF),
            vm((2, 512, 256), BF),
            vm((2, 512, 256), BF),
            vm((2, 512, 256), BF),
            vm((2, 2, 512, 256), BF),
            vm((4, 16, WA, 256), BF),
            vm((2, 8, 2, 2, WB, 256), BF),
            vm((2, 3, 8, WA, 256), BF),
            vm((8, 2, WA, 256), BF),
            vm((2, 2, 2, WB, 256), BF),
            vm((2, 2, 3, 2, 2, WB, 256), BF),
            vm((2, WA, 256), BF),
            vm((2, 3, 2, WA, 256), BF),
            vm((2, 2, 2, WB, 256), BF),
            vm((2, WA, 256), BF),
            vm((8, WB, 256), BF),
            vm((4, 128, 256), BF),
            dma((5,)),
            dma((5,)), dma((5,)),
            dma((2, 3)), dma((2, 3)),
            dma((2, 3)), dma((2, 3)),
            dma((2, 2, 4)), dma((2, 2, 4)),
            dma((2, 4)), dma((2, 4)),
            dma((2,)), dma((2,)),
            dma((2, 2, 2)), dma((8,)),
            dma((4,)), dma((4,)),
        ],
        compiler_params=pltpu.CompilerParams(
            collective_id=0, has_side_effects=True, vmem_limit_bytes=48 << 20
        ),
        cost_estimate=pl.CostEstimate(
            flops=4_800_000_000, bytes_accessed=10 << 20, transcendentals=32768
        ),
    )(activations, cotangent, projector, first_moment, second_moment)


def solution(mesh):
    return jax.shard_map(
        body,
        mesh=mesh,
        in_specs=(
            P("fsdp", "tp"),
            P("fsdp", "tp"),
            P(None, "tp"),
            P("fsdp", "tp"),
            P("fsdp", "tp"),
        ),
        out_specs=(P("tp", "fsdp"), P("fsdp", "tp"), P("fsdp", "tp")),
        check_vma=False,
    )
```

```python
import jax
import jax.numpy as jnp
from jax import lax
from jax.experimental import pallas as pl
from jax.experimental.pallas import tpu as pltpu
from jax.sharding import PartitionSpec as P

MESH = pl.DeviceIdType.MESH
BF, F32 = jnp.bfloat16, jnp.float32
WA = 64
WB = 128 - WA
SHARED = 352
DIRECT = 2048 - 4 * SHARED
NEAR = 256


def device(x, y_hi, z, t):
    return (x * 16 + y_hi * 8 + z, t)


def kernel(
    a_hbm, c_hbm, p_hbm, m1_hbm, m2_hbm,
    w_out, f_out, s_out,
    a_v, c_v, ct_v, p_own, p_v, m1_v, m2_v,
    hold, core_out, core_in, y_out, y_in, proj,
    ga, gb, xin, fa, zb1, zb2, za1, za2, fb, ra, rb, dirs,
    lsem, pcsend, pcrecv, pysend, pyrecv, prsend, prrecv, esend, erecv, xsend, xrecv,
    zbsend, zbrecv, zasend, zarecv, rasend, rarecv, rbsend, rbrecv, dsend, drecv,
):
    f = lax.axis_index("fsdp")
    t = lax.axis_index("tp")
    x, y_hi, z = f // 16, (f // 8) % 2, f % 8
    y_lo, c = t // 2, t % 2
    near_y = y_hi * 2 + 1 - y_lo
    other_y = lax.rem(y_hi * 2 + y_lo + jnp.where(y_lo == 0, 3, 1), 4)

    def at_side(side, core):
        yy = near_y if side == 0 else other_y
        return device(x, yy // 2, z, (yy % 2) * 2 + core)

    def at_x(d):
        return device(lax.rem(x + (1 if d == 0 else 3), 4), y_hi, z, t)

    def at_z(d):
        return device(x, y_hi, lax.rem(z + (1 if d == 0 else 7), 8), t)

    other_core = device(x, y_hi, z, y_lo * 2 + 1 - c)
    y_partner = device(x, y_hi, z, (1 - y_lo) * 2 + c)

    def remote(src, dst, ss, rs, dev):
        return pltpu.make_async_remote_copy(
            src_ref=src, dst_ref=dst, send_sem=ss, recv_sem=rs, device_id=dev, device_id_type=MESH
        )

    own_rows = pl.ds(pl.multiple_of(t * 2048, 2048), 2048)
    loads = [
        pltpu.make_async_copy(p_hbm, p_own, lsem.at[0]),
        pltpu.make_async_copy(a_hbm, a_v, lsem.at[1]),
        pltpu.make_async_copy(c_hbm, c_v, lsem.at[2]),
        pltpu.make_async_copy(p_hbm.at[own_rows, pl.ds(0, 128)], p_v.at[0, t], lsem.at[3]),
        pltpu.make_async_copy(p_hbm.at[own_rows, pl.ds(128, 128)], p_v.at[1, t], lsem.at[4]),
        pltpu.make_async_copy(m1_hbm, m1_v, lsem.at[5]),
        pltpu.make_async_copy(m2_hbm, m2_v, lsem.at[6]),
    ]
    for load in loads:
        load.start()

    barrier = pltpu.get_barrier_semaphore()
    partners = [other_core, at_x(0), at_x(1), at_z(0), at_z(1)]
    partners += [at_side(s, k) for s in range(2) for k in range(2)]
    for dev in partners:
        pl.semaphore_signal(barrier, inc=1, device_id=dev, device_id_type=MESH)
    for xs in range(4):
        for yh in range(2):
            @pl.when(jnp.logical_not((xs == x) & (x == t) & (yh == y_hi)))
            def _():
                pl.semaphore_signal(
                    barrier, inc=1, device_id=device(xs, yh, z, x), device_id_type=MESH
                )

    pl.semaphore_wait(barrier, len(partners) + 8 - jnp.where(x == t, 1, 0))

    def p_core(h):
        rows = pl.ds(pl.multiple_of((y_lo * 2 + 1 - c) * 2048, 2048), 2048)
        return remote(
            p_own.at[rows, pl.ds(h * 128, 128)], p_v.at[h, t], pcsend.at[h], pcrecv.at[h], other_core
        )

    def rows_of(kind, side, other):
        if kind == 2:
            return pl.ds(4 * SHARED + side * NEAR, NEAR if side == 0 else DIRECT - NEAR)
        parity = z % 2 if kind == 0 else x % 2
        if other:
            parity = 1 - parity
        base = kind * 2 * SHARED + parity * SHARED + side * (SHARED // 2)
        return pl.ds(pl.multiple_of(base, 16), SHARED // 2)

    def p_y(h, kind, side, core):
        rows = rows_of(kind, side, False)
        target = (1 - y_lo) * 2 + core
        src = pl.ds(pl.multiple_of(target * 2048 + rows.start, 16), rows.size)
        return remote(
            p_own.at[src, pl.ds(h * 128, 128)], p_v.at[h, t, rows],
            pysend.at[h, kind, side, core], pyrecv.at[h, kind, side, c], at_side(side, core),
        )

    def p_y_wait(h, kind, side, core):
        slot = p_v.at[h, (1 - y_lo) * 2 + core, rows_of(kind, side, False)]
        remote(slot, slot, pysend.at[h, kind, side, core], pyrecv.at[h, kind, side, core], other_core).wait_recv()

    def p_relay(h, kind, side, core):
        slot = p_v.at[h, (1 - y_lo) * 2 + core, rows_of(kind, side, False)]
        return remote(
            slot, slot, prsend.at[h, kind, side, core], prrecv.at[h, kind, side, core],
            at_z(side) if kind == 0 else at_x(side),
        )

    def p_relay_wait(h, kind, side, core):
        slot = p_v.at[h, (1 - y_lo) * 2 + core, rows_of(kind, side, True)]
        remote(slot, slot, prsend.at[h, kind, side, core], prrecv.at[h, kind, side, core], other_core).wait_recv()

    each = [(core, kind, side) for core in range(2) for kind in range(2) for side in range(2)]

    whole = [(core, 2, side) for core in range(2) for side in range(2)]

    def p_first(h):
        for core, kind, side in each:
            p_y(h, kind, side, core).start()

    def p_second(h):
        for core, kind, side in each:
            p_y(h, kind, side, core).wait_send()
        for core, kind, side in whole:
            p_y(h, kind, side, core).start()

    def p_relays(h):
        for core, kind, side in each:
            p_y_wait(h, kind, side, core)
            p_relay(h, kind, side, core).start()

    def p_arrive(h):
        for core, kind, side in whole:
            p_y_wait(h, kind, side, core)
        for core, kind, side in each:
            p_relay_wait(h, kind, side, core)

    def slot_of(e):
        return y_lo if e == 0 else 1 - y_lo

    def to_core(h, e):
        return remote(core_out.at[h, e], core_in.at[h, e], esend.at[0, h, e], erecv.at[0, h, e], other_core)

    def to_y(h, e):
        return remote(
            y_out.at[h, e], y_in.at[h, 1 - e], esend.at[1, h, e], erecv.at[1, h, 1 - e], y_partner
        )

    def y_wait(h, e):
        remote(y_out.at[h, e], y_in.at[h, e], esend.at[1, h, e], erecv.at[1, h, e], y_partner).wait_recv()

    def share(h, e):
        block = proj.at[h, slot_of(e) * 2 + c]
        return remote(block, block, esend.at[2, h, e], erecv.at[2, h, e], other_core)

    def share_wait(h, e):
        block = proj.at[h, slot_of(e) * 2 + 1 - c]
        remote(block, block, esend.at[2, h, e], erecv.at[2, h, e], other_core).wait_recv()

    def partial(h, e):
        s = slot_of(e)
        weights = jnp.concatenate([p_v[h, s * 2], p_v[h, s * 2 + 1]], axis=1)
        acc = jnp.dot(a_v[...], weights, preferred_element_type=F32)
        low, high = acc[:, :128], acc[:, 128:]
        hold[h, e] = jnp.where(c == 0, low, high)
        core_out[h, e] = jnp.where(c == 0, high, low).astype(BF)
        to_core(h, e).start()

    def chip_sum(h, e):
        to_core(h, e).wait_recv()
        total = hold[h, e] + core_in[h, e].astype(F32)
        hold[h, e] = total
        y_out[h, e] = total.astype(BF)

    def finish(h, e):
        y_wait(h, e)
        proj[h, slot_of(e) * 2 + c] = (hold[h, e] + y_in[h, e].astype(F32)).astype(BF)
        share(h, e).start()

    def gradient(h, e):
        share_wait(h, e)
        s = slot_of(e)

        @pl.loop(0, 4)
        def _(i):
            rows = pl.ds(pl.multiple_of(i * 512, 512), 512)
            right = jnp.concatenate([proj[h, s * 2], proj[h, s * 2 + 1]], axis=1)
            acc = jnp.dot(ct_v[rows, :], right, preferred_element_type=F32).astype(BF)
            blocks = acc.reshape(4, 128, 256)
            for k in range(4):
                for q in range(2):
                    part = blocks[k, :, q * 128:(q + 1) * 128]
                    ga[h, s * 2 + q, i * 4 + k] = part[:WA]
                    gb[h, (i % 2) * 4 + k, i // 2, s * 2 + q] = part[WA:]

    def add(ref, *others):
        total = ref[...].astype(F32)
        for other in others:
            total = total + other[...].astype(F32)
        ref[...] = total.astype(BF)

    def xq(d, n):
        return lax.rem(x + (n if d == 0 else 4 - n), 4)

    def x_msg(h, d, m):
        q, half = (xq(d, 2), d) if m == 0 else (xq(d, 1), 1 - d) if m == 1 else (xq(d, 1), d)
        src = ga.at[h, q, pl.ds(half * 8, 8)]
        return remote(src, xin.at[h, d, m], xsend.at[h, d, m], xrecv.at[h, d, m], at_x(d))

    def x_start(h):
        for d in range(2):
            x_msg(h, d, 0).start()

    def x_next(h):
        for d in range(2):
            x_msg(h, d, 0).wait_send()
            x_msg(h, d, 1).start()

    def x_sum(h):
        for d in range(2):
            x_msg(h, d, 0).wait_recv()
            add(ga.at[h, xq(d, 1), pl.ds(d * 8, 8)], xin.at[h, d, 0])
            x_msg(h, d, 2).start()

    def x_end(h):
        for d in range(2):
            x_msg(h, d, 1).wait_recv()
        for d in range(2):
            x_msg(h, d, 2).wait_recv()
        for yh in range(2):
            for k in range(8):
                fa[h, k, yh] = (
                    ga[h, x, yh * 8 + k].astype(F32)
                    + xin[h, yh, 2, k].astype(F32)
                    + xin[h, 1 - yh, 1, k].astype(F32)
                ).astype(BF)
        for d in range(2):
            z_msg(za, h, d, 0).start()

    def zc(d, n):
        return lax.rem(z + (n if d == 0 else 8 - n), 8)

    zb = (gb, zb1, zb2, zbsend, zbrecv)
    za = (fa, za1, za2, zasend, zarecv)

    def z_msg(ring, h, d, m):
        data, first, later, ss, rs = ring
        if m == 0:
            src, dst = data.at[h, zc(d, 4), d], first.at[h, d]
        else:
            src, dst = data.at[h, zc(d, 4 - m)], later.at[h, d, m - 1]
        return remote(src, dst, ss.at[h, d, m], rs.at[h, d, m], at_z(d))

    def z_start(ring, h):
        for d in range(2):
            z_msg(ring, h, d, 0).start()

    def z_step(ring, h, m):
        data, first, later, _, _ = ring
        for d in range(2):
            z_msg(ring, h, d, m - 1).wait_recv()
            if m == 1:
                add(data.at[h, zc(d, 3), d], first.at[h, d])
            else:
                add(data.at[h, zc(d, 4 - m)], later.at[h, d, m - 2])
            z_msg(ring, h, d, m).start()

    def mine(yh, q):
        return (x == t) & (yh == y_hi) & (q == t)

    def ra_msg(h, yh):
        return remote(
            fa.at[h, z, yh], ra.at[h, y_hi], rasend.at[h, yh], rarecv.at[h, y_hi], device(t, yh, z, x)
        )

    def rb_msg(h, q, yh):
        s = x * 2 + y_hi
        return remote(
            fb.at[h, yh, q], rb.at[h, s], rbsend.at[h, q, yh], rbrecv.at[h, s], device(t, yh, z, q)
        )

    def zb_end(h):
        for d in range(2):
            z_msg(zb, h, d, 3).wait_recv()
        fb[h] = (
            gb[h, z].astype(F32) + zb2[h, 0, 2].astype(F32) + zb2[h, 1, 2].astype(F32)
        ).astype(BF)
        for q in range(4):
            for yh in range(2):
                own = mine(yh, q)

                @pl.when(own)
                def _():
                    rb[h, x * 2 + y_hi] = fb[h, yh, q]

                @pl.when(jnp.logical_not(own))
                def _():
                    rb_msg(h, q, yh).start()

    def za_end(h):
        for d in range(2):
            z_msg(za, h, d, 3).wait_recv()
        add(fa.at[h, z], za2.at[h, 0, 2], za2.at[h, 1, 2])
        for yh in range(2):
            own = mine(yh, x)

            @pl.when(own)
            def _():
                ra[h, y_hi] = fa[h, z, yh]

            @pl.when(jnp.logical_not(own))
            def _():
                ra_msg(h, yh).start()

    def d_msg(h, k):
        return remote(
            dirs.at[h, t], dirs.at[h, t], dsend.at[h, k], drecv.at[h, k], (f, lax.rem(t + k, 4))
        )

    def adam(h):
        for xs in range(4):
            for yh in range(2):
                s = xs * 2 + yh

                @pl.when(jnp.logical_not((xs == x) & (x == t) & (yh == y_hi)))
                def _():
                    remote(rb.at[h, s], rb.at[h, s], rbsend.at[h, 0, 0], rbrecv.at[h, s], other_core).wait_recv()
        for yh in range(2):
            @pl.when(jnp.logical_not(mine(yh, x)))
            def _():
                remote(ra.at[h, yh], ra.at[h, yh], rasend.at[h, 0], rarecv.at[h, yh], other_core).wait_recv()
        up = ra[h, 0].astype(F32) + ra[h, 1].astype(F32)
        down = rb[h, 0].astype(F32)
        for s in range(1, 8):
            down = down + rb[h, s].astype(F32)
        cols = pl.ds(h * 128, 128)
        for rows, g in ((pl.ds(0, WA), up), (pl.ds(WA, WB), down)):
            first_new = 0.9 * m1_v[rows, cols] + 0.1 * g
            second_new = 0.999 * m2_v[rows, cols] + 0.001 * g * g
            f_out[rows, cols] = first_new
            s_out[rows, cols] = second_new
            dirs[h, t, rows, :] = (first_new / (jnp.sqrt(second_new) + 1e-08)).astype(BF)
        for k in (1, 2, 3):
            d_msg(h, k).start()

    def update(h):
        for k in (1, 2, 3):
            slot = dirs.at[h, lax.rem(t + 4 - k, 4)]
            remote(slot, slot, dsend.at[h, k], drecv.at[h, k], other_core).wait_recv()

        @pl.loop(0, 4)
        def _(i):
            rows = pl.ds(pl.multiple_of(i * 512, 512), 512)
            left = jnp.concatenate([p_v[h, q, rows, :] for q in range(4)], axis=1)
            right = jnp.concatenate([dirs[h, q] for q in range(4)], axis=1)
            acc = lax.dot_general(left, right, (((1,), (1,)), ((), ())), preferred_element_type=F32)
            if h == 0:
                w_out[rows, :] = acc
            else:
                w_out[rows, :] = w_out[rows, :] + acc

    loads[0].wait()
    p_first(0)
    p_core(0).start()
    p_core(1).start()
    loads[2].wait()

    @pl.loop(0, 4)
    def _(i):
        o = pl.multiple_of(i * 512, 512)
        ct_v[pl.ds(o, 512), :] = c_v[:, pl.ds(o, 512)].T

    p_second(0)
    loads[1].wait()
    loads[3].wait()
    p_core(0).wait_recv()
    partial(0, 0)
    p_relays(0)
    chip_sum(0, 0)
    to_y(0, 0).start()
    loads[4].wait()
    p_core(1).wait_recv()
    partial(1, 0)
    chip_sum(1, 0)
    p_arrive(0)
    p_first(1)
    partial(0, 1)
    chip_sum(0, 1)
    to_y(0, 1).start()
    finish(0, 1)
    p_second(1)
    gradient(0, 1)
    p_relays(1)
    finish(0, 0)
    to_y(1, 0).start()
    gradient(0, 0)
    x_start(0)
    z_start(zb, 0)
    p_arrive(1)
    partial(1, 1)
    chip_sum(1, 1)
    to_y(1, 1).start()
    finish(1, 1)
    x_next(0)
    z_step(zb, 0, 1)
    gradient(1, 1)
    x_sum(0)
    finish(1, 0)
    z_step(zb, 0, 2)
    gradient(1, 0)
    x_start(1)
    z_start(zb, 1)
    x_end(0)
    z_step(zb, 0, 3)
    x_next(1)
    z_step(zb, 1, 1)
    x_sum(1)
    z_step(za, 0, 1)
    zb_end(0)
    z_step(zb, 1, 2)
    z_step(za, 0, 2)
    x_end(1)
    z_step(zb, 1, 3)
    z_step(za, 0, 3)
    z_step(za, 1, 1)
    za_end(0)
    z_step(za, 1, 2)
    zb_end(1)
    z_step(za, 1, 3)
    loads[5].wait()
    loads[6].wait()
    adam(0)
    za_end(1)
    update(0)
    adam(1)
    update(1)

    for h in range(2):
        p_core(h).wait_send()
        for core, kind, side in whole:
            p_y(h, kind, side, core).wait_send()
        for core, kind, side in each:
            p_relay(h, kind, side, core).wait_send()
        for e in range(2):
            to_core(h, e).wait_send()
            to_y(h, e).wait_send()
            share(h, e).wait_send()
        for d in range(2):
            for m in (1, 2):
                x_msg(h, d, m).wait_send()
            for m in range(4):
                z_msg(zb, h, d, m).wait_send()
                z_msg(za, h, d, m).wait_send()
        for yh in range(2):
            @pl.when(jnp.logical_not(mine(yh, x)))
            def _():
                ra_msg(h, yh).wait_send()

            for q in range(4):
                @pl.when(jnp.logical_not(mine(yh, q)))
                def _():
                    rb_msg(h, q, yh).wait_send()
        for k in (1, 2, 3):
            d_msg(h, k).wait_send()


def body(activations, cotangent, projector, first_moment, second_moment):
    dma = pltpu.SemaphoreType.DMA
    vm = pltpu.VMEM
    return pl.pallas_call(
        kernel,
        name="galore_step",
        out_shape=(
            jax.ShapeDtypeStruct((2048, 128), F32),
            jax.ShapeDtypeStruct((128, 256), F32),
            jax.ShapeDtypeStruct((128, 256), F32),
        ),
        in_specs=[pl.BlockSpec(memory_space=pltpu.HBM)] * 5,
        out_specs=(pl.BlockSpec(memory_space=pltpu.VMEM),) * 3,
        scratch_shapes=[
            vm((512, 2048), BF),
            vm((512, 2048), BF),
            vm((2048, 512), BF),
            vm((8192, 256), BF),
            vm((2, 4, 2048, 128), BF),
            vm((128, 256), F32),
            vm((128, 256), F32),
            vm((2, 2, 512, 128), F32),
            vm((2, 2, 512, 128), BF),
            vm((2, 2, 512, 128), BF),
            vm((2, 2, 512, 128), BF),
            vm((2, 2, 512, 128), BF),
            vm((2, 4, 512, 128), BF),
            vm((2, 4, 16, WA, 128), BF),
            vm((2, 8, 2, 4, WB, 128), BF),
            vm((2, 2, 3, 8, WA, 128), BF),
            vm((2, 8, 2, WA, 128), BF),
            vm((2, 2, 4, WB, 128), BF),
            vm((2, 2, 3, 2, 4, WB, 128), BF),
            vm((2, 2, WA, 128), BF),
            vm((2, 2, 3, 2, WA, 128), BF),
            vm((2, 2, 4, WB, 128), BF),
            vm((2, 2, WA, 128), BF),
            vm((2, 8, WB, 128), BF),
            vm((2, 4, 128, 128), BF),
            dma((7,)),
            dma((2,)), dma((2,)),
            dma((2, 3, 2, 2)), dma((2, 3, 2, 2)),
            dma((2, 2, 2, 2)), dma((2, 2, 2, 2)),
            dma((3, 2, 2)), dma((3, 2, 2)),
            dma((2, 2, 3)), dma((2, 2, 3)),
            dma((2, 2, 4)), dma((2, 2, 4)),
            dma((2, 2, 4)), dma((2, 2, 4)),
            dma((2, 2)), dma((2, 2)),
            dma((2, 4, 2)), dma((2, 8)),
            dma((2, 4)), dma((2, 4)),
        ],
        compiler_params=pltpu.CompilerParams(
            collective_id=0, has_side_effects=True, vmem_limit_bytes=60 << 20
        ),
        cost_estimate=pl.CostEstimate(
            flops=4_800_000_000, bytes_accessed=10 << 20, transcendentals=32768
        ),
    )(activations, cotangent, projector, first_moment, second_moment)


def solution(mesh):
    return jax.shard_map(
        body,
        mesh=mesh,
        in_specs=(
            P("fsdp", "tp"),
            P("fsdp", "tp"),
            P(None, "tp"),
            P("fsdp", "tp"),
            P("fsdp", "tp"),
        ),
        out_specs=(P("tp", "fsdp"), P("fsdp", "tp"), P("fsdp", "tp")),
        check_vma=False,
    )
```

```python
import jax
import jax.numpy as jnp
from jax import lax
from jax.experimental import pallas as pl
from jax.experimental.pallas import tpu as pltpu
from jax.sharding import PartitionSpec as P

MESH = pl.DeviceIdType.MESH
BF, F32 = jnp.bfloat16, jnp.float32
WA = 64
WB = 128 - WA
SHARED = 352
DIRECT = 2048 - 4 * SHARED
NEAR_SHARED = (144, 112)
NEAR_DIRECT = (256, 208)


def device(x, y_hi, z, t):
    return (x * 16 + y_hi * 8 + z, t)


def kernel(
    a_hbm, c_hbm, p_hbm, m1_hbm, m2_hbm,
    w_out, f_out, s_out,
    a_v, c_v, ct_v, p_own, p_v, m1_v, m2_v,
    hold, core_out, core_in, y_out, y_in, proj,
    ga, gb, xin, fa, zb1, zb2, za1, za2, fb, ra, rb, dirs,
    lsem, pcsend, pcrecv, pysend, pyrecv, prsend, prrecv, esend, erecv, xsend, xrecv,
    zbsend, zbrecv, zasend, zarecv, rasend, rarecv, rbsend, rbrecv, dsend, drecv,
):
    f = lax.axis_index("fsdp")
    t = lax.axis_index("tp")
    x, y_hi, z = f // 16, (f // 8) % 2, f % 8
    y_lo, c = t // 2, t % 2
    near_y = y_hi * 2 + 1 - y_lo
    other_y = lax.rem(y_hi * 2 + y_lo + jnp.where(y_lo == 0, 3, 1), 4)

    def at_side(side, core):
        yy = near_y if side == 0 else other_y
        return device(x, yy // 2, z, (yy % 2) * 2 + core)

    def at_x(d):
        return device(lax.rem(x + (1 if d == 0 else 3), 4), y_hi, z, t)

    def at_z(d):
        return device(x, y_hi, lax.rem(z + (1 if d == 0 else 7), 8), t)

    other_core = device(x, y_hi, z, y_lo * 2 + 1 - c)
    y_partner = device(x, y_hi, z, (1 - y_lo) * 2 + c)

    def remote(src, dst, ss, rs, dev):
        return pltpu.make_async_remote_copy(
            src_ref=src, dst_ref=dst, send_sem=ss, recv_sem=rs, device_id=dev, device_id_type=MESH
        )

    own_rows = pl.ds(pl.multiple_of(t * 2048, 2048), 2048)
    loads = [
        pltpu.make_async_copy(p_hbm, p_own, lsem.at[0]),
        pltpu.make_async_copy(a_hbm, a_v, lsem.at[1]),
        pltpu.make_async_copy(c_hbm, c_v, lsem.at[2]),
        pltpu.make_async_copy(p_hbm.at[own_rows, pl.ds(0, 128)], p_v.at[0, t], lsem.at[3]),
        pltpu.make_async_copy(p_hbm.at[own_rows, pl.ds(128, 128)], p_v.at[1, t], lsem.at[4]),
        pltpu.make_async_copy(m1_hbm, m1_v, lsem.at[5]),
        pltpu.make_async_copy(m2_hbm, m2_v, lsem.at[6]),
    ]
    loads[0].start()

    barrier = pltpu.get_barrier_semaphore()
    partners = [other_core, at_x(0), at_x(1), at_z(0), at_z(1)]
    partners += [at_side(s, k) for s in range(2) for k in range(2)]
    for dev in partners:
        pl.semaphore_signal(barrier, inc=1, device_id=dev, device_id_type=MESH)
    for xs in range(4):
        for yh in range(2):
            @pl.when(jnp.logical_not((xs == x) & (x == t) & (yh == y_hi)))
            def _():
                pl.semaphore_signal(
                    barrier, inc=1, device_id=device(xs, yh, z, x), device_id_type=MESH
                )

    pl.semaphore_wait(barrier, len(partners) + 8 - jnp.where(x == t, 1, 0))

    def p_core(h):
        rows = pl.ds(pl.multiple_of((y_lo * 2 + 1 - c) * 2048, 2048), 2048)
        return remote(
            p_own.at[rows, pl.ds(h * 128, 128)], p_v.at[h, t], pcsend.at[h], pcrecv.at[h], other_core
        )

    def rows_of(h, kind, side, other):
        whole_rows, near_rows = (DIRECT, NEAR_DIRECT[h]) if kind == 2 else (SHARED, NEAR_SHARED[h])
        size = near_rows if side == 0 else whole_rows - near_rows
        if kind == 2:
            return pl.ds(4 * SHARED + side * near_rows, size)
        parity = z % 2 if kind == 0 else x % 2
        if other:
            parity = 1 - parity
        return pl.ds(pl.multiple_of(kind * 2 * SHARED + parity * SHARED + side * near_rows, 16), size)

    def p_y(h, kind, side, core):
        rows = rows_of(h, kind, side, False)
        target = (1 - y_lo) * 2 + core
        src = pl.ds(pl.multiple_of(target * 2048 + rows.start, 16), rows.size)
        return remote(
            p_own.at[src, pl.ds(h * 128, 128)], p_v.at[h, t, rows],
            pysend.at[h, kind, side, core], pyrecv.at[h, kind, side, c], at_side(side, core),
        )

    def p_y_wait(h, kind, side, core):
        slot = p_v.at[h, (1 - y_lo) * 2 + core, rows_of(h, kind, side, False)]
        remote(slot, slot, pysend.at[h, kind, side, core], pyrecv.at[h, kind, side, core], other_core).wait_recv()

    def p_relay(h, kind, side, core):
        slot = p_v.at[h, (1 - y_lo) * 2 + core, rows_of(h, kind, side, False)]
        return remote(
            slot, slot, prsend.at[h, kind, side, core], prrecv.at[h, kind, side, core],
            at_z((side + core) % 2) if kind == 0 else at_x((side + core) % 2),
        )

    def p_relay_wait(h, kind, side, core):
        slot = p_v.at[h, (1 - y_lo) * 2 + core, rows_of(h, kind, side, True)]
        remote(slot, slot, prsend.at[h, kind, side, core], prrecv.at[h, kind, side, core], other_core).wait_recv()

    each = [(core, kind, side) for core in range(2) for kind in range(2) for side in range(2)]

    whole = [(core, 2, side) for core in range(2) for side in range(2)]

    def p_first(h):
        for core, kind, side in each:
            p_y(h, kind, side, core).start()

    def p_second(h):
        for core, kind, side in each:
            p_y(h, kind, side, core).wait_send()
        for core, kind, side in whole:
            p_y(h, kind, side, core).start()

    def p_relays(h):
        for core, kind, side in each:
            p_y_wait(h, kind, side, core)
            p_relay(h, kind, side, core).start()

    def p_arrive(h):
        for core, kind, side in whole:
            p_y_wait(h, kind, side, core)
        for core, kind, side in each:
            p_relay_wait(h, kind, side, core)

    def slot_of(e):
        return y_lo if e == 0 else 1 - y_lo

    def to_core(h, e):
        return remote(core_out.at[h, e], core_in.at[h, e], esend.at[0, h, e], erecv.at[0, h, e], other_core)

    def to_y(h, e):
        return remote(
            y_out.at[h, e], y_in.at[h, 1 - e], esend.at[1, h, e], erecv.at[1, h, 1 - e], y_partner
        )

    def y_wait(h, e):
        remote(y_out.at[h, e], y_in.at[h, e], esend.at[1, h, e], erecv.at[1, h, e], y_partner).wait_recv()

    def share(h, e):
        block = proj.at[h, slot_of(e) * 2 + c]
        return remote(block, block, esend.at[2, h, e], erecv.at[2, h, e], other_core)

    def share_wait(h, e):
        block = proj.at[h, slot_of(e) * 2 + 1 - c]
        remote(block, block, esend.at[2, h, e], erecv.at[2, h, e], other_core).wait_recv()

    def partial(h, e):
        s = slot_of(e)
        weights = jnp.concatenate([p_v[h, s * 2], p_v[h, s * 2 + 1]], axis=1)
        acc = jnp.dot(a_v[...], weights, preferred_element_type=F32)
        low, high = acc[:, :128], acc[:, 128:]
        hold[h, e] = jnp.where(c == 0, low, high)
        core_out[h, e] = jnp.where(c == 0, high, low).astype(BF)
        to_core(h, e).start()

    def chip_sum(h, e):
        to_core(h, e).wait_recv()
        total = hold[h, e] + core_in[h, e].astype(F32)
        hold[h, e] = total
        y_out[h, e] = total.astype(BF)

    def finish(h, e):
        y_wait(h, e)
        proj[h, slot_of(e) * 2 + c] = (hold[h, e] + y_in[h, e].astype(F32)).astype(BF)
        share(h, e).start()

    def gradient(h, e):
        share_wait(h, e)
        s = slot_of(e)

        @pl.loop(0, 4)
        def _(i):
            rows = pl.ds(pl.multiple_of(i * 512, 512), 512)
            right = jnp.concatenate([proj[h, s * 2], proj[h, s * 2 + 1]], axis=1)
            acc = jnp.dot(ct_v[rows, :], right, preferred_element_type=F32).astype(BF)
            blocks = acc.reshape(4, 128, 256)
            for k in range(4):
                for q in range(2):
                    part = blocks[k, :, q * 128:(q + 1) * 128]
                    ga[h, s * 2 + q, i * 4 + k] = part[:WA]
                    gb[h, (i % 2) * 4 + k, i // 2, s * 2 + q] = part[WA:]

    def add(ref, *others):
        total = ref[...].astype(F32)
        for other in others:
            total = total + other[...].astype(F32)
        ref[...] = total.astype(BF)

    def xq(d, n):
        return lax.rem(x + (n if d == 0 else 4 - n), 4)

    def x_msg(h, d, m):
        q, half = (xq(d, 2), d) if m == 0 else (xq(d, 1), 1 - d) if m == 1 else (xq(d, 1), d)
        src = ga.at[h, q, pl.ds(half * 8, 8)]
        return remote(src, xin.at[h, d, m], xsend.at[h, d, m], xrecv.at[h, d, m], at_x(d))

    def x_start(h):
        for d in range(2):
            x_msg(h, d, 0).start()

    def x_next(h):
        for d in range(2):
            x_msg(h, d, 0).wait_send()
            x_msg(h, d, 1).start()

    def x_sum(h):
        for d in range(2):
            x_msg(h, d, 0).wait_recv()
            add(ga.at[h, xq(d, 1), pl.ds(d * 8, 8)], xin.at[h, d, 0])
            x_msg(h, d, 2).start()

    def x_end(h):
        for d in range(2):
            x_msg(h, d, 1).wait_recv()
        for d in range(2):
            x_msg(h, d, 2).wait_recv()
        for yh in range(2):
            for k in range(8):
                fa[h, k, yh] = (
                    ga[h, x, yh * 8 + k].astype(F32)
                    + xin[h, yh, 2, k].astype(F32)
                    + xin[h, 1 - yh, 1, k].astype(F32)
                ).astype(BF)
        for d in range(2):
            z_msg(za, h, d, 0).start()

    def zc(d, n):
        return lax.rem(z + (n if d == 0 else 8 - n), 8)

    zb = (gb, zb1, zb2, zbsend, zbrecv)
    za = (fa, za1, za2, zasend, zarecv)

    def z_msg(ring, h, d, m):
        data, first, later, ss, rs = ring
        if m == 0:
            src, dst = data.at[h, zc(d, 4), d], first.at[h, d]
        else:
            src, dst = data.at[h, zc(d, 4 - m)], later.at[h, d, m - 1]
        return remote(src, dst, ss.at[h, d, m], rs.at[h, d, m], at_z(d))

    def z_start(ring, h):
        for d in range(2):
            z_msg(ring, h, d, 0).start()

    def z_step(ring, h, m):
        data, first, later, _, _ = ring
        for d in range(2):
            z_msg(ring, h, d, m - 1).wait_recv()
            if m == 1:
                add(data.at[h, zc(d, 3), d], first.at[h, d])
            else:
                add(data.at[h, zc(d, 4 - m)], later.at[h, d, m - 2])
            z_msg(ring, h, d, m).start()

    def mine(yh, q):
        return (x == t) & (yh == y_hi) & (q == t)

    def ra_msg(h, yh):
        return remote(
            fa.at[h, z, yh], ra.at[h, y_hi], rasend.at[h, yh], rarecv.at[h, y_hi], device(t, yh, z, x)
        )

    def rb_msg(h, q, yh):
        s = x * 2 + y_hi
        return remote(
            fb.at[h, yh, q], rb.at[h, s], rbsend.at[h, q, yh], rbrecv.at[h, s], device(t, yh, z, q)
        )

    def zb_end(h):
        for d in range(2):
            z_msg(zb, h, d, 3).wait_recv()
        fb[h] = (
            gb[h, z].astype(F32) + zb2[h, 0, 2].astype(F32) + zb2[h, 1, 2].astype(F32)
        ).astype(BF)
        for q in range(4):
            for yh in range(2):
                own = mine(yh, q)

                @pl.when(own)
                def _():
                    rb[h, x * 2 + y_hi] = fb[h, yh, q]

                @pl.when(jnp.logical_not(own))
                def _():
                    rb_msg(h, q, yh).start()

    def za_end(h):
        for d in range(2):
            z_msg(za, h, d, 3).wait_recv()
        add(fa.at[h, z], za2.at[h, 0, 2], za2.at[h, 1, 2])
        for yh in range(2):
            own = mine(yh, x)

            @pl.when(own)
            def _():
                ra[h, y_hi] = fa[h, z, yh]

            @pl.when(jnp.logical_not(own))
            def _():
                ra_msg(h, yh).start()

    def d_msg(h, k):
        return remote(
            dirs.at[h, t], dirs.at[h, t], dsend.at[h, k], drecv.at[h, k], (f, lax.rem(t + k, 4))
        )

    def adam(h):
        for xs in range(4):
            for yh in range(2):
                s = xs * 2 + yh

                @pl.when(jnp.logical_not((xs == x) & (x == t) & (yh == y_hi)))
                def _():
                    remote(rb.at[h, s], rb.at[h, s], rbsend.at[h, 0, 0], rbrecv.at[h, s], other_core).wait_recv()
        for yh in range(2):
            @pl.when(jnp.logical_not(mine(yh, x)))
            def _():
                remote(ra.at[h, yh], ra.at[h, yh], rasend.at[h, 0], rarecv.at[h, yh], other_core).wait_recv()
        up = ra[h, 0].astype(F32) + ra[h, 1].astype(F32)
        down = rb[h, 0].astype(F32)
        for s in range(1, 8):
            down = down + rb[h, s].astype(F32)
        cols = pl.ds(h * 128, 128)
        for rows, g in ((pl.ds(0, WA), up), (pl.ds(WA, WB), down)):
            first_new = 0.9 * m1_v[rows, cols] + 0.1 * g
            second_new = 0.999 * m2_v[rows, cols] + 0.001 * g * g
            f_out[rows, cols] = first_new
            s_out[rows, cols] = second_new
            dirs[h, t, rows, :] = (first_new / (jnp.sqrt(second_new) + 1e-08)).astype(BF)
        for k in (1, 2, 3):
            d_msg(h, k).start()

    def update(h):
        for k in (1, 2, 3):
            slot = dirs.at[h, lax.rem(t + 4 - k, 4)]
            remote(slot, slot, dsend.at[h, k], drecv.at[h, k], other_core).wait_recv()

        @pl.loop(0, 4)
        def _(i):
            rows = pl.ds(pl.multiple_of(i * 512, 512), 512)
            left = jnp.concatenate([p_v[h, q, rows, :] for q in range(4)], axis=1)
            right = jnp.concatenate([dirs[h, q] for q in range(4)], axis=1)
            acc = lax.dot_general(left, right, (((1,), (1,)), ((), ())), preferred_element_type=F32)
            if h == 0:
                w_out[rows, :] = acc
            else:
                w_out[rows, :] = w_out[rows, :] + acc

    loads[0].wait()
    p_first(0)
    for load in (loads[2], loads[1], *loads[3:]):
        load.start()
    p_core(0).start()
    p_core(1).start()
    loads[2].wait()

    @pl.loop(0, 4)
    def _(i):
        o = pl.multiple_of(i * 512, 512)
        ct_v[pl.ds(o, 512), :] = c_v[:, pl.ds(o, 512)].T

    p_second(0)
    loads[1].wait()
    loads[3].wait()
    p_core(0).wait_recv()
    partial(0, 0)
    p_relays(0)
    chip_sum(0, 0)
    to_y(0, 0).start()
    loads[4].wait()
    p_core(1).wait_recv()
    partial(1, 0)
    chip_sum(1, 0)
    p_arrive(0)
    p_first(1)
    partial(0, 1)
    chip_sum(0, 1)
    to_y(0, 1).start()
    finish(0, 1)
    p_second(1)
    gradient(0, 1)
    p_relays(1)
    finish(0, 0)
    to_y(1, 0).start()
    gradient(0, 0)
    x_start(0)
    z_start(zb, 0)
    p_arrive(1)
    partial(1, 1)
    chip_sum(1, 1)
    to_y(1, 1).start()
    finish(1, 1)
    x_next(0)
    z_step(zb, 0, 1)
    gradient(1, 1)
    x_sum(0)
    finish(1, 0)
    z_step(zb, 0, 2)
    gradient(1, 0)
    x_start(1)
    z_start(zb, 1)
    x_end(0)
    z_step(zb, 0, 3)
    x_next(1)
    z_step(zb, 1, 1)
    z_step(za, 0, 1)
    x_sum(1)
    zb_end(0)
    z_step(za, 0, 2)
    z_step(zb, 1, 2)
    x_end(1)
    z_step(za, 0, 3)
    z_step(za, 1, 1)
    z_step(zb, 1, 3)
    za_end(0)
    z_step(za, 1, 2)
    zb_end(1)
    z_step(za, 1, 3)
    loads[5].wait()
    loads[6].wait()
    adam(0)
    za_end(1)
    update(0)
    adam(1)
    update(1)

    for h in range(2):
        p_core(h).wait_send()
        for core, kind, side in whole:
            p_y(h, kind, side, core).wait_send()
        for core, kind, side in each:
            p_relay(h, kind, side, core).wait_send()
        for e in range(2):
            to_core(h, e).wait_send()
            to_y(h, e).wait_send()
            share(h, e).wait_send()
        for d in range(2):
            for m in (1, 2):
                x_msg(h, d, m).wait_send()
            for m in range(4):
                z_msg(zb, h, d, m).wait_send()
                z_msg(za, h, d, m).wait_send()
        for yh in range(2):
            @pl.when(jnp.logical_not(mine(yh, x)))
            def _():
                ra_msg(h, yh).wait_send()

            for q in range(4):
                @pl.when(jnp.logical_not(mine(yh, q)))
                def _():
                    rb_msg(h, q, yh).wait_send()
        for k in (1, 2, 3):
            d_msg(h, k).wait_send()


def body(activations, cotangent, projector, first_moment, second_moment):
    dma = pltpu.SemaphoreType.DMA
    vm = pltpu.VMEM
    return pl.pallas_call(
        kernel,
        name="galore_step",
        out_shape=(
            jax.ShapeDtypeStruct((2048, 128), F32),
            jax.ShapeDtypeStruct((128, 256), F32),
            jax.ShapeDtypeStruct((128, 256), F32),
        ),
        in_specs=[pl.BlockSpec(memory_space=pltpu.HBM)] * 5,
        out_specs=(pl.BlockSpec(memory_space=pltpu.VMEM),) * 3,
        scratch_shapes=[
            vm((512, 2048), BF),
            vm((512, 2048), BF),
            vm((2048, 512), BF),
            vm((8192, 256), BF),
            vm((2, 4, 2048, 128), BF),
            vm((128, 256), F32),
            vm((128, 256), F32),
            vm((2, 2, 512, 128), F32),
            vm((2, 2, 512, 128), BF),
            vm((2, 2, 512, 128), BF),
            vm((2, 2, 512, 128), BF),
            vm((2, 2, 512, 128), BF),
            vm((2, 4, 512, 128), BF),
            vm((2, 4, 16, WA, 128), BF),
            vm((2, 8, 2, 4, WB, 128), BF),
            vm((2, 2, 3, 8, WA, 128), BF),
            vm((2, 8, 2, WA, 128), BF),
            vm((2, 2, 4, WB, 128), BF),
            vm((2, 2, 3, 2, 4, WB, 128), BF),
            vm((2, 2, WA, 128), BF),
            vm((2, 2, 3, 2, WA, 128), BF),
            vm((2, 2, 4, WB, 128), BF),
            vm((2, 2, WA, 128), BF),
            vm((2, 8, WB, 128), BF),
            vm((2, 4, 128, 128), BF),
            dma((7,)),
            dma((2,)), dma((2,)),
            dma((2, 3, 2, 2)), dma((2, 3, 2, 2)),
            dma((2, 2, 2, 2)), dma((2, 2, 2, 2)),
            dma((3, 2, 2)), dma((3, 2, 2)),
            dma((2, 2, 3)), dma((2, 2, 3)),
            dma((2, 2, 4)), dma((2, 2, 4)),
            dma((2, 2, 4)), dma((2, 2, 4)),
            dma((2, 2)), dma((2, 2)),
            dma((2, 4, 2)), dma((2, 8)),
            dma((2, 4)), dma((2, 4)),
        ],
        compiler_params=pltpu.CompilerParams(
            collective_id=0, has_side_effects=True, vmem_limit_bytes=60 << 20
        ),
        cost_estimate=pl.CostEstimate(
            flops=4_800_000_000, bytes_accessed=10 << 20, transcendentals=32768
        ),
    )(activations, cotangent, projector, first_moment, second_moment)


def solution(mesh):
    return jax.shard_map(
        body,
        mesh=mesh,
        in_specs=(
            P("fsdp", "tp"),
            P("fsdp", "tp"),
            P(None, "tp"),
            P("fsdp", "tp"),
            P("fsdp", "tp"),
        ),
        out_specs=(P("tp", "fsdp"), P("fsdp", "tp"), P("fsdp", "tp")),
        check_vma=False,
    )
```

```python
import jax
import jax.numpy as jnp
from jax import lax
from jax.experimental import pallas as pl
from jax.experimental.pallas import tpu as pltpu
from jax.sharding import PartitionSpec as P

MESH = pl.DeviceIdType.MESH
BF, F32 = jnp.bfloat16, jnp.float32
WA = 64
WB = 128 - WA
SHARED = 352
DIRECT = 2048 - 4 * SHARED
NEAR_SHARED = (144, 112)
NEAR_DIRECT = (256, 208)


def device(x, y_hi, z, t):
    return (x * 16 + y_hi * 8 + z, t)


def kernel(
    a_hbm, c_hbm, p_hbm, m1_hbm, m2_hbm,
    w_out, f_out, s_out,
    a_v, c_v, ct_v, p_own, p_v, m1_v, m2_v,
    hold, core_out, core_in, y_out, y_in, proj,
    ga, gb, xin, fa, zb1, zb2, za1, za2, fb, ra, rb, dirs,
    lsem, pcsend, pcrecv, pysend, pyrecv, prsend, prrecv, esend, erecv, xsend, xrecv,
    zbsend, zbrecv, zasend, zarecv, rasend, rarecv, rbsend, rbrecv, dsend, drecv,
):
    f = lax.axis_index("fsdp")
    t = lax.axis_index("tp")
    x, y_hi, z = f // 16, (f // 8) % 2, f % 8
    y_lo, c = t // 2, t % 2
    near_y = y_hi * 2 + 1 - y_lo
    other_y = lax.rem(y_hi * 2 + y_lo + jnp.where(y_lo == 0, 3, 1), 4)

    def at_side(side, core):
        yy = near_y if side == 0 else other_y
        return device(x, yy // 2, z, (yy % 2) * 2 + core)

    def at_x(d):
        return device(lax.rem(x + (1 if d == 0 else 3), 4), y_hi, z, t)

    def at_z(d):
        return device(x, y_hi, lax.rem(z + (1 if d == 0 else 7), 8), t)

    other_core = device(x, y_hi, z, y_lo * 2 + 1 - c)
    y_partner = device(x, y_hi, z, (1 - y_lo) * 2 + c)

    def remote(src, dst, ss, rs, dev):
        return pltpu.make_async_remote_copy(
            src_ref=src, dst_ref=dst, send_sem=ss, recv_sem=rs, device_id=dev, device_id_type=MESH
        )

    own_rows = pl.ds(pl.multiple_of(t * 2048, 2048), 2048)
    loads = [
        pltpu.make_async_copy(p_hbm, p_own, lsem.at[0]),
        pltpu.make_async_copy(a_hbm, a_v, lsem.at[1]),
        pltpu.make_async_copy(c_hbm, c_v, lsem.at[2]),
        pltpu.make_async_copy(p_hbm.at[own_rows, pl.ds(0, 128)], p_v.at[0, t], lsem.at[3]),
        pltpu.make_async_copy(p_hbm.at[own_rows, pl.ds(128, 128)], p_v.at[1, t], lsem.at[4]),
        pltpu.make_async_copy(m1_hbm, m1_v, lsem.at[5]),
        pltpu.make_async_copy(m2_hbm, m2_v, lsem.at[6]),
    ]
    loads[0].start()

    barrier = pltpu.get_barrier_semaphore()
    partners = [other_core, at_x(0), at_x(1), at_z(0), at_z(1)]
    partners += [at_side(s, k) for s in range(2) for k in range(2)]
    for dev in partners:
        pl.semaphore_signal(barrier, inc=1, device_id=dev, device_id_type=MESH)
    for xs in range(4):
        for yh in range(2):
            @pl.when(jnp.logical_not((xs == x) & (x == t) & (yh == y_hi)))
            def _():
                pl.semaphore_signal(
                    barrier, inc=1, device_id=device(xs, yh, z, x), device_id_type=MESH
                )

    pl.semaphore_wait(barrier, len(partners) + 8 - jnp.where(x == t, 1, 0))

    def p_core(h):
        rows = pl.ds(pl.multiple_of((y_lo * 2 + 1 - c) * 2048, 2048), 2048)
        return remote(
            p_own.at[rows, pl.ds(h * 128, 128)], p_v.at[h, t], pcsend.at[h], pcrecv.at[h], other_core
        )

    def rows_of(h, kind, side, other):
        whole_rows, near_rows = (DIRECT, NEAR_DIRECT[h]) if kind == 2 else (SHARED, NEAR_SHARED[h])
        size = near_rows if side == 0 else whole_rows - near_rows
        if kind == 2:
            return pl.ds(4 * SHARED + side * near_rows, size)
        parity = z % 2 if kind == 0 else x % 2
        if other:
            parity = 1 - parity
        return pl.ds(pl.multiple_of(kind * 2 * SHARED + parity * SHARED + side * near_rows, 16), size)

    def p_y(h, kind, side, core):
        rows = rows_of(h, kind, side, False)
        target = (1 - y_lo) * 2 + core
        src = pl.ds(pl.multiple_of(target * 2048 + rows.start, 16), rows.size)
        return remote(
            p_own.at[src, pl.ds(h * 128, 128)], p_v.at[h, t, rows],
            pysend.at[h, kind, side, core], pyrecv.at[h, kind, side, c], at_side(side, core),
        )

    def p_y_wait(h, kind, side, core):
        slot = p_v.at[h, (1 - y_lo) * 2 + core, rows_of(h, kind, side, False)]
        remote(slot, slot, pysend.at[h, kind, side, core], pyrecv.at[h, kind, side, core], other_core).wait_recv()

    def p_relay(h, kind, side, core):
        slot = p_v.at[h, (1 - y_lo) * 2 + core, rows_of(h, kind, side, False)]
        return remote(
            slot, slot, prsend.at[h, kind, side, core], prrecv.at[h, kind, side, core],
            at_z((side + core) % 2) if kind == 0 else at_x((side + core) % 2),
        )

    def p_relay_wait(h, kind, side, core):
        slot = p_v.at[h, (1 - y_lo) * 2 + core, rows_of(h, kind, side, True)]
        remote(slot, slot, prsend.at[h, kind, side, core], prrecv.at[h, kind, side, core], other_core).wait_recv()

    each = [(core, kind, side) for core in range(2) for kind in range(2) for side in range(2)]

    whole = [(core, 2, side) for core in range(2) for side in range(2)]

    def p_first(h):
        for core, kind, side in each:
            p_y(h, kind, side, core).start()

    def p_second(h):
        for core, kind, side in each:
            p_y(h, kind, side, core).wait_send()
        for core, kind, side in whole:
            p_y(h, kind, side, core).start()

    def p_relays(h):
        for core, kind, side in each:
            p_y_wait(h, kind, side, core)
            p_relay(h, kind, side, core).start()

    def p_arrive(h):
        for core, kind, side in whole:
            p_y_wait(h, kind, side, core)
        for core, kind, side in each:
            p_relay_wait(h, kind, side, core)

    def slot_of(e):
        return y_lo if e == 0 else 1 - y_lo

    def to_core(h, e):
        return remote(core_out.at[h, e], core_in.at[h, e], esend.at[0, h, e], erecv.at[0, h, e], other_core)

    def to_y(h, e):
        return remote(
            y_out.at[h, e], y_in.at[h, 1 - e], esend.at[1, h, e], erecv.at[1, h, 1 - e], y_partner
        )

    def y_wait(h, e):
        remote(y_out.at[h, e], y_in.at[h, e], esend.at[1, h, e], erecv.at[1, h, e], y_partner).wait_recv()

    def share(h, e):
        block = proj.at[h, slot_of(e) * 2 + c]
        return remote(block, block, esend.at[2, h, e], erecv.at[2, h, e], other_core)

    def share_wait(h, e):
        block = proj.at[h, slot_of(e) * 2 + 1 - c]
        remote(block, block, esend.at[2, h, e], erecv.at[2, h, e], other_core).wait_recv()

    def partial(h, e):
        s = slot_of(e)
        weights = jnp.concatenate([p_v[h, s * 2], p_v[h, s * 2 + 1]], axis=1)
        acc = jnp.dot(a_v[...], weights, preferred_element_type=F32)
        low, high = acc[:, :128], acc[:, 128:]
        hold[h, e] = jnp.where(c == 0, low, high)
        core_out[h, e] = jnp.where(c == 0, high, low).astype(BF)
        to_core(h, e).start()

    def chip_sum(h, e):
        to_core(h, e).wait_recv()
        total = hold[h, e] + core_in[h, e].astype(F32)
        hold[h, e] = total
        y_out[h, e] = total.astype(BF)

    def finish(h, e):
        y_wait(h, e)
        proj[h, slot_of(e) * 2 + c] = (hold[h, e] + y_in[h, e].astype(F32)).astype(BF)
        share(h, e).start()

    def gradient(h, e):
        share_wait(h, e)
        s = slot_of(e)

        @pl.loop(0, 4)
        def _(i):
            rows = pl.ds(pl.multiple_of(i * 512, 512), 512)
            right = jnp.concatenate([proj[h, s * 2], proj[h, s * 2 + 1]], axis=1)
            acc = jnp.dot(ct_v[rows, :], right, preferred_element_type=F32).astype(BF)
            blocks = acc.reshape(4, 128, 256)
            for k in range(4):
                for q in range(2):
                    part = blocks[k, :, q * 128:(q + 1) * 128]
                    ga[h, s * 2 + q, i * 4 + k] = part[:WA]
                    gb[h, (i % 2) * 4 + k, i // 2, s * 2 + q] = part[WA:]

    def add(ref, *others):
        total = ref[...].astype(F32)
        for other in others:
            total = total + other[...].astype(F32)
        ref[...] = total.astype(BF)

    def xq(d, n):
        return lax.rem(x + (n if d == 0 else 4 - n), 4)

    def x_msg(h, d, m):
        q, half = (xq(d, 2), d) if m == 0 else (xq(d, 1), 1 - d) if m == 1 else (xq(d, 1), d)
        src = ga.at[h, q, pl.ds(half * 8, 8)]
        return remote(src, xin.at[h, d, m], xsend.at[h, d, m], xrecv.at[h, d, m], at_x(d))

    def x_start(h):
        for d in range(2):
            x_msg(h, d, 0).start()

    def x_next(h):
        for d in range(2):
            x_msg(h, d, 0).wait_send()
            x_msg(h, d, 1).start()

    def x_sum(h):
        for d in range(2):
            x_msg(h, d, 0).wait_recv()
            add(ga.at[h, xq(d, 1), pl.ds(d * 8, 8)], xin.at[h, d, 0])
            x_msg(h, d, 2).start()

    def x_end(h):
        for d in range(2):
            x_msg(h, d, 1).wait_recv()
        for d in range(2):
            x_msg(h, d, 2).wait_recv()
        for yh in range(2):
            for k in range(8):
                fa[h, k, yh] = (
                    ga[h, x, yh * 8 + k].astype(F32)
                    + xin[h, yh, 2, k].astype(F32)
                    + xin[h, 1 - yh, 1, k].astype(F32)
                ).astype(BF)
        z_start(za, h)

    def zc(d, n):
        return lax.rem(z + (n if d == 0 else 8 - n), 8)

    zb = (gb, zb1, zb2, zbsend, zbrecv)
    za = (fa, za1, za2, zasend, zarecv)

    def z_msg(ring, h, d, m):
        data, first, later, ss, rs = ring
        if m == 0:
            src, dst = data.at[h, zc(d, 4), d], first.at[h, d]
        elif m in (1, 4):
            half = d if m == 1 else 1 - d
            src, dst = data.at[h, zc(d, 3), half], later.at[h, d, 0, half]
        else:
            src, dst = data.at[h, zc(d, 4 - m)], later.at[h, d, m - 1]
        return remote(src, dst, ss.at[h, d, m], rs.at[h, d, m], at_z(d))

    def z_start(ring, h):
        for d in range(2):
            z_msg(ring, h, d, 0).start()
        for d in range(2):
            z_msg(ring, h, d, 4).start()

    def z_step(ring, h, m):
        data, first, later, _, _ = ring
        for d in range(2):
            z_msg(ring, h, d, m - 1).wait_recv()
            if m == 2:
                z_msg(ring, h, d, 4).wait_recv()
            if m == 1:
                add(data.at[h, zc(d, 3), d], first.at[h, d])
            else:
                add(data.at[h, zc(d, 4 - m)], later.at[h, d, m - 2])
            z_msg(ring, h, d, m).start()

    def mine(yh, q):
        return (x == t) & (yh == y_hi) & (q == t)

    def ra_msg(h, yh):
        return remote(
            fa.at[h, z, yh], ra.at[h, y_hi], rasend.at[h, yh], rarecv.at[h, y_hi], device(t, yh, z, x)
        )

    def rb_msg(h, q, yh):
        s = x * 2 + y_hi
        return remote(
            fb.at[h, yh, q], rb.at[h, s], rbsend.at[h, q, yh], rbrecv.at[h, s], device(t, yh, z, q)
        )

    def zb_end(h):
        for d in range(2):
            z_msg(zb, h, d, 3).wait_recv()
        fb[h] = (
            gb[h, z].astype(F32) + zb2[h, 0, 2].astype(F32) + zb2[h, 1, 2].astype(F32)
        ).astype(BF)
        for q in range(4):
            for yh in range(2):
                own = mine(yh, q)

                @pl.when(own)
                def _():
                    rb[h, x * 2 + y_hi] = fb[h, yh, q]

                @pl.when(jnp.logical_not(own))
                def _():
                    rb_msg(h, q, yh).start()

    def za_end(h):
        for d in range(2):
            z_msg(za, h, d, 3).wait_recv()
        add(fa.at[h, z], za2.at[h, 0, 2], za2.at[h, 1, 2])
        for yh in range(2):
            own = mine(yh, x)

            @pl.when(own)
            def _():
                ra[h, y_hi] = fa[h, z, yh]

            @pl.when(jnp.logical_not(own))
            def _():
                ra_msg(h, yh).start()

    def d_msg(h, k):
        return remote(
            dirs.at[h, t], dirs.at[h, t], dsend.at[h, k], drecv.at[h, k], (f, lax.rem(t + k, 4))
        )

    def adam(h):
        for xs in range(4):
            for yh in range(2):
                s = xs * 2 + yh

                @pl.when(jnp.logical_not((xs == x) & (x == t) & (yh == y_hi)))
                def _():
                    remote(rb.at[h, s], rb.at[h, s], rbsend.at[h, 0, 0], rbrecv.at[h, s], other_core).wait_recv()
        for yh in range(2):
            @pl.when(jnp.logical_not(mine(yh, x)))
            def _():
                remote(ra.at[h, yh], ra.at[h, yh], rasend.at[h, 0], rarecv.at[h, yh], other_core).wait_recv()
        up = ra[h, 0].astype(F32) + ra[h, 1].astype(F32)
        down = rb[h, 0].astype(F32)
        for s in range(1, 8):
            down = down + rb[h, s].astype(F32)
        cols = pl.ds(h * 128, 128)
        for rows, g in ((pl.ds(0, WA), up), (pl.ds(WA, WB), down)):
            first_new = 0.9 * m1_v[rows, cols] + 0.1 * g
            second_new = 0.999 * m2_v[rows, cols] + 0.001 * g * g
            f_out[rows, cols] = first_new
            s_out[rows, cols] = second_new
            dirs[h, t, rows, :] = (first_new / (jnp.sqrt(second_new) + 1e-08)).astype(BF)
        for k in (1, 2, 3):
            d_msg(h, k).start()

    def update(h):
        for k in (1, 2, 3):
            slot = dirs.at[h, lax.rem(t + 4 - k, 4)]
            remote(slot, slot, dsend.at[h, k], drecv.at[h, k], other_core).wait_recv()

        @pl.loop(0, 4)
        def _(i):
            rows = pl.ds(pl.multiple_of(i * 512, 512), 512)
            left = jnp.concatenate([p_v[h, q, rows, :] for q in range(4)], axis=1)
            right = jnp.concatenate([dirs[h, q] for q in range(4)], axis=1)
            acc = lax.dot_general(left, right, (((1,), (1,)), ((), ())), preferred_element_type=F32)
            if h == 0:
                w_out[rows, :] = acc
            else:
                w_out[rows, :] = w_out[rows, :] + acc

    loads[0].wait()
    p_first(0)
    for load in (loads[2], loads[1], *loads[3:]):
        load.start()
    p_core(0).start()
    p_core(1).start()
    loads[2].wait()

    @pl.loop(0, 4)
    def _(i):
        o = pl.multiple_of(i * 512, 512)
        ct_v[pl.ds(o, 512), :] = c_v[:, pl.ds(o, 512)].T

    p_second(0)
    loads[1].wait()
    loads[3].wait()
    p_core(0).wait_recv()
    partial(0, 0)
    p_relays(0)
    chip_sum(0, 0)
    to_y(0, 0).start()
    loads[4].wait()
    p_core(1).wait_recv()
    partial(1, 0)
    chip_sum(1, 0)
    p_arrive(0)
    p_first(1)
    partial(0, 1)
    chip_sum(0, 1)
    to_y(0, 1).start()
    finish(0, 1)
    p_second(1)
    gradient(0, 1)
    p_relays(1)
    finish(0, 0)
    to_y(1, 0).start()
    gradient(0, 0)
    x_start(0)
    z_start(zb, 0)
    p_arrive(1)
    partial(1, 1)
    chip_sum(1, 1)
    to_y(1, 1).start()
    finish(1, 1)
    x_next(0)
    z_step(zb, 0, 1)
    gradient(1, 1)
    x_sum(0)
    finish(1, 0)
    z_step(zb, 0, 2)
    gradient(1, 0)
    x_start(1)
    z_start(zb, 1)
    x_end(0)
    z_step(zb, 0, 3)
    x_next(1)
    z_step(zb, 1, 1)
    z_step(za, 0, 1)
    x_sum(1)
    zb_end(0)
    z_step(za, 0, 2)
    z_step(zb, 1, 2)
    x_end(1)
    z_step(za, 0, 3)
    z_step(za, 1, 1)
    z_step(zb, 1, 3)
    za_end(0)
    z_step(za, 1, 2)
    zb_end(1)
    z_step(za, 1, 3)
    loads[5].wait()
    loads[6].wait()
    adam(0)
    za_end(1)
    update(0)
    adam(1)
    update(1)

    for h in range(2):
        p_core(h).wait_send()
        for core, kind, side in whole:
            p_y(h, kind, side, core).wait_send()
        for core, kind, side in each:
            p_relay(h, kind, side, core).wait_send()
        for e in range(2):
            to_core(h, e).wait_send()
            to_y(h, e).wait_send()
            share(h, e).wait_send()
        for d in range(2):
            for m in (1, 2):
                x_msg(h, d, m).wait_send()
            for m in range(5):
                z_msg(zb, h, d, m).wait_send()
                z_msg(za, h, d, m).wait_send()
        for yh in range(2):
            @pl.when(jnp.logical_not(mine(yh, x)))
            def _():
                ra_msg(h, yh).wait_send()

            for q in range(4):
                @pl.when(jnp.logical_not(mine(yh, q)))
                def _():
                    rb_msg(h, q, yh).wait_send()
        for k in (1, 2, 3):
            d_msg(h, k).wait_send()


def body(activations, cotangent, projector, first_moment, second_moment):
    dma = pltpu.SemaphoreType.DMA
    vm = pltpu.VMEM
    return pl.pallas_call(
        kernel,
        name="galore_step",
        out_shape=(
            jax.ShapeDtypeStruct((2048, 128), F32),
            jax.ShapeDtypeStruct((128, 256), F32),
            jax.ShapeDtypeStruct((128, 256), F32),
        ),
        in_specs=[pl.BlockSpec(memory_space=pltpu.HBM)] * 5,
        out_specs=(pl.BlockSpec(memory_space=pltpu.VMEM),) * 3,
        scratch_shapes=[
            vm((512, 2048), BF),
            vm((512, 2048), BF),
            vm((2048, 512), BF),
            vm((8192, 256), BF),
            vm((2, 4, 2048, 128), BF),
            vm((128, 256), F32),
            vm((128, 256), F32),
            vm((2, 2, 512, 128), F32),
            vm((2, 2, 512, 128), BF),
            vm((2, 2, 512, 128), BF),
            vm((2, 2, 512, 128), BF),
            vm((2, 2, 512, 128), BF),
            vm((2, 4, 512, 128), BF),
            vm((2, 4, 16, WA, 128), BF),
            vm((2, 8, 2, 4, WB, 128), BF),
            vm((2, 2, 3, 8, WA, 128), BF),
            vm((2, 8, 2, WA, 128), BF),
            vm((2, 2, 4, WB, 128), BF),
            vm((2, 2, 3, 2, 4, WB, 128), BF),
            vm((2, 2, WA, 128), BF),
            vm((2, 2, 3, 2, WA, 128), BF),
            vm((2, 2, 4, WB, 128), BF),
            vm((2, 2, WA, 128), BF),
            vm((2, 8, WB, 128), BF),
            vm((2, 4, 128, 128), BF),
            dma((7,)),
            dma((2,)), dma((2,)),
            dma((2, 3, 2, 2)), dma((2, 3, 2, 2)),
            dma((2, 2, 2, 2)), dma((2, 2, 2, 2)),
            dma((3, 2, 2)), dma((3, 2, 2)),
            dma((2, 2, 3)), dma((2, 2, 3)),
            dma((2, 2, 5)), dma((2, 2, 5)),
            dma((2, 2, 5)), dma((2, 2, 5)),
            dma((2, 2)), dma((2, 2)),
            dma((2, 4, 2)), dma((2, 8)),
            dma((2, 4)), dma((2, 4)),
        ],
        compiler_params=pltpu.CompilerParams(
            collective_id=0, has_side_effects=True, vmem_limit_bytes=60 << 20
        ),
        cost_estimate=pl.CostEstimate(
            flops=4_800_000_000, bytes_accessed=10 << 20, transcendentals=32768
        ),
    )(activations, cotangent, projector, first_moment, second_moment)


def solution(mesh):
    return jax.shard_map(
        body,
        mesh=mesh,
        in_specs=(
            P("fsdp", "tp"),
            P("fsdp", "tp"),
            P(None, "tp"),
            P("fsdp", "tp"),
            P("fsdp", "tp"),
        ),
        out_specs=(P("tp", "fsdp"), P("fsdp", "tp"), P("fsdp", "tp")),
        check_vma=False,
    )
```
